256 devices in a mesh: dp: 32 (over z, y), tensor: 8 (over x, core).
Axes of the slice: x: 4, y: 4, z: 8, core: 2. Of those that a mesh axis runs over, the one named last changes fastest.
Arguments:
- saved_inputs: bfloat16 [2, 65536, 3584], P(None, 'dp'), may hold values from -6 to 6
- kv_cotangent: bfloat16 [2, 65536, 2048], P(None, 'dp', 'tensor'), may hold values from -0.125 to 0.125
- error_buffer: bfloat16 [32, 2, 3584, 2048], P('dp', None, None, 'tensor'), may hold values from -3 to 3
- q_start: float32 [2, 32, 2048], P(None, None, 'tensor'), may hold values from -0.125 to 0.125
Outputs:
- new_error: bfloat16 [32, 2, 3584, 2048], P('dp', None, None, 'tensor')
- q_factor: float32 [2, 32, 2048], P(None, None, 'tensor')
The draws below stay inside these ranges and needn't reach their ends.
All inputs are finite; a program needn't handle non-finite values.
Results may differ from the reference program's by a relative error of at most 0.001.
Values sent between devices are 32-bit elements; how exact they have to be, the bound alone decides.
A program may use at most 128 MiB of HBM per device.

```python
import jax
import jax.numpy as jnp
from jax import lax

FEATS = 3584
RANK = 32
LAYERS = 2
TOK_DEV = 2048
COLS = 2048
REPLICAS = 32
TOKENS = 65536
N_DP = 32


def levels(stream_key, dims, split, least, top_value):
    level = 1.0
    for position, shards_of in split:
        heights = jax.random.uniform(jax.random.fold_in(jax.random.fold_in(stream_key, 6), position), (shards_of,), jnp.float32, least / len(split), top_value / len(split))
        level = level * jnp.repeat(jnp.exp(heights), dims[position] // shards_of).reshape((-1,) + (1,) * (len(dims) - 1 - position))
    return level


def centred(stream_key, dims, width, bound, cuts=(), kind=jnp.bfloat16):
    values = width * jax.random.normal(stream_key, dims, jnp.float32)
    if cuts:
        values = values * levels(stream_key, dims, cuts, -0.22, 0.18)
    return jnp.clip(values, -bound, bound).astype(kind)


def setup_inputs(seed: int = 0) -> dict:
    key_of = jax.random.split(jax.random.key(seed), 5)
    return {
        "saved_inputs": centred(key_of[0], (LAYERS, TOKENS, FEATS), 1.0, 6.0, ((1, 32),)),
        "kv_cotangent": centred(key_of[1], (LAYERS, TOKENS, COLS), TOK_DEV ** -0.5, 0.125, ((1, 32), (2, 8))),
        "error_buffer": centred(key_of[2], (REPLICAS, LAYERS, FEATS, COLS), 0.5, 3.0, ((0, 32), (3, 8))),
        "q_start": centred(key_of[3], (LAYERS, RANK, COLS), COLS ** -0.5, 0.125, ((2, 8),), jnp.float32),
    }


highest_precision = lax.Precision.HIGHEST

def replica_merged(saved_inputs, kv_cotangent, error_buffer, replica):
    start = (replica * TOK_DEV).astype(jnp.int32)
    row_block = lax.dynamic_slice_in_dim(saved_inputs, start, TOK_DEV, 1).astype(jnp.float32)
    cot_block = lax.dynamic_slice_in_dim(kv_cotangent, start, TOK_DEV, 1).astype(jnp.float32)
    weight_gradient = jnp.einsum('ltf,ltc->lfc', row_block, cot_block)
    own_error = lax.dynamic_index_in_dim(error_buffer, replica, 0, keepdims=False)
    return weight_gradient + own_error.astype(jnp.float32)

def reference(saved_inputs, kv_cotangent, error_buffer, q_start):
    replica_ids = jnp.arange(REPLICAS, dtype=jnp.int32)

    def accumulate_into(summed, replica):
        return (summed + replica_merged(saved_inputs, kv_cotangent, error_buffer, replica), None)
    summed0 = jnp.zeros((LAYERS, FEATS, COLS), jnp.float32)
    summed, unused = lax.scan(accumulate_into, summed0, replica_ids)
    left_factor_matrix = jnp.einsum('lrc,lfc->lrf', q_start, summed, precision=highest_precision)
    gram_product = jnp.einsum('xwe,xpe->xwp', left_factor_matrix, left_factor_matrix, precision=highest_precision)
    lower_factor = jnp.linalg.cholesky(gram_product)
    ortho_factor = lax.linalg.triangular_solve(lower_factor, left_factor_matrix, left_side=True, lower=True)
    q_factor = jnp.einsum('lrf,lfc->lrc', ortho_factor, summed, precision=highest_precision) / N_DP
    decompressed = jnp.einsum('lrf,lrc->lfc', ortho_factor, q_factor, precision=highest_precision)

    def updated(replica):
        merged = replica_merged(saved_inputs, kv_cotangent, error_buffer, replica)
        return (merged - decompressed).astype(jnp.bfloat16)
    new_error = lax.map(updated, replica_ids)
    return (new_error, q_factor)
```

```python
import functools

import jax
import jax.numpy as jnp
from jax import lax
from jax.experimental import pallas as pl
from jax.experimental.pallas import tpu as pltpu
from jax.sharding import PartitionSpec as P

MESH = pl.DeviceIdType.MESH
F32, BF16 = jnp.float32, jnp.bfloat16
FEATS, RANK, LAYERS, TOK, COLS = 3584, 32, 2, 2048, 256
NZ, NY, NX = 8, 4, 4
HALF = TOK // 2
BLK = 128
NBLK = FEATS // BLK
OWN = NBLK // 2
GRAD_F = 512


def mm(a, b, ca=1, cb=0, precision=None):
    return lax.dot_general(a, b, (((ca,), (cb,)), ((), ())), precision=precision, preferred_element_type=F32)


def split3(v):
    hi = v.astype(BF16)
    rest = v - hi.astype(F32)
    mid = rest.astype(BF16)
    lo = (rest - mid.astype(F32)).astype(BF16)
    return jnp.concatenate([hi, mid, lo], axis=0)


def fold3(r):
    return r[0:RANK] + r[RANK : 2 * RANK] + r[2 * RANK : 3 * RANK]


def kernel(
    s_hbm, k_hbm, e_hbm, q_hbm, err_hbm, qf_hbm,
    s, k, e, qv, q3, m, hi, lo, ot, zl, zr, z3, pp, cr, ps, xr, zs, pf, gl, ub, yr, zq, qt, qo,
    hs, out_sem, z_s, z_r, c_s, c_r, xy_s, xy_r, zz_s, zz_r, ag_s, ag_r, ac_s, ac_r, y1_s, y1_r, qz_s, qz_r, y2_s, y2_r,
):
    dp, t = lax.axis_index("dp"), lax.axis_index("tensor")
    z, y, x, c = dp // NY, dp % NY, t // 2, t % 2
    xy = y * NX + x

    def dev(z_, y_, x_, c_):
        return (z_ * NY + y_, x_ * 2 + c_)

    partner = dev(z, y, x, 1 - c)

    def xy_peer(j):
        return (y + j // NX) % NY, (x + j % NX) % NX

    def remote(src, dst, ss, rs, device):
        return pltpu.make_async_remote_copy(
            src_ref=src, dst_ref=dst, send_sem=ss, recv_sem=rs, device_id=device, device_id_type=MESH
        )

    def wait_recv(ref, ss, rs):
        remote(ref, ref, ss, rs, partner).wait_recv()

    def wait_send(ref, ss, rs):
        remote(ref, ref, ss, rs, partner).wait_send()

    barrier = pltpu.get_barrier_semaphore()
    pl.semaphore_signal(barrier, inc=1, device_id=partner, device_id_type=MESH)

    def greet_z(j, _):
        pl.semaphore_signal(barrier, inc=1, device_id=dev((z + j) % NZ, y, x, c), device_id_type=MESH)
        return 0

    def greet_xy(j, _):
        ny, nx = xy_peer(j)
        pl.semaphore_signal(barrier, inc=1, device_id=dev(z, ny, nx, c), device_id_type=MESH)
        return 0

    lax.fori_loop(1, NZ, greet_z, 0)
    lax.fori_loop(1, NX * NY, greet_xy, 0)

    def half_copy(hbm, vmem, l, part, sem):
        rows = pl.ds(pl.multiple_of((c if part == 0 else 1 - c) * HALF, HALF), HALF)
        return pltpu.make_async_copy(hbm.at[l, rows], vmem.at[l, pl.ds(part * HALF, HALF)], sem)

    cq = pltpu.make_async_copy(q_hbm, qv, hs.at[0])
    ck = [[half_copy(k_hbm, k, l, h, hs.at[1 + 2 * l + h]) for h in range(2)] for l in range(LAYERS)]
    ce = [pltpu.make_async_copy(e_hbm.at[0, l], e.at[l], hs.at[5 + l]) for l in range(LAYERS)]
    cs = [[half_copy(s_hbm, s, l, h, hs.at[7 + 2 * l + h]) for h in range(2)] for l in range(LAYERS)]
    cq.start()
    for l in range(LAYERS):
        ck[l][0].start()
        ck[l][1].start()
    ce[0].start()
    ce[1].start()
    cs[0][0].start()

    cq.wait()
    for l in range(LAYERS):
        q3[l] = split3(qv[l])
    for l in range(LAYERS):
        ck[l][0].wait()
        ck[l][1].wait()
        for h in range(2):
            zl[l, h] = fold3(mm(q3[l], k[l, pl.ds(h * HALF, HALF), :], 1, 1))
    cs[1][0].start()

    def error_part(l):
        def step(i, _):
            r = fold3(mm(q3[l], e[l, pl.ds(pl.multiple_of(i * 512, 512), 512), :], 1, 1))
            for j in range(4):
                pp[l, i * 4 + j] = r[:, j * BLK : (j + 1) * BLK]
            return 0

        ce[l].wait()
        lax.fori_loop(0, FEATS // 512, step, 0)

    error_part(0)

    pl.semaphore_wait(barrier, 1 + (NZ - 1) + (NX * NY - 1))
    for l in range(LAYERS):
        remote(zl.at[l, 1], zr.at[l], z_s.at[l], z_r.at[l], partner).start()
    error_part(1)
    cs[0][1].start()
    cs[1][1].start()

    def p_blocks(l, side):
        def step(i, _):
            b0 = side * OWN + i * 7
            f0 = pl.multiple_of(b0 * BLK, BLK)
            r = fold3(mm(z3[l], s[l, pl.ds(0, HALF), pl.ds(f0, 7 * BLK)]))
            for j in range(7):
                pp[l, b0 + j] += r[:, j * BLK : (j + 1) * BLK]
            return 0

        lax.fori_loop(0, 2, step, 0)

    def p_term(l):
        wait_recv(zr.at[l], z_s.at[l], z_r.at[l])
        z3[l] = split3(zl[l, 0] + zr[l])
        cs[l][0].wait()
        p_blocks(l, 1 - c)
        remote(pp.at[l, pl.ds((1 - c) * OWN, OWN)], cr.at[l], c_s.at[l], c_r.at[l], partner).start()
        p_blocks(l, c)

    def add_cores(l):
        wait_recv(cr.at[l], c_s.at[l], c_r.at[l])

        def step(b, _):
            ps[l, b] = pp[l, c * OWN + b] + cr[l, b]
            return 0

        lax.fori_loop(0, OWN, step, 0)

        def send(j, _):
            ny, nx = xy_peer(j)
            b = ny * NX + nx - 2 * l

            @pl.when((b >= 0) & (b < OWN))
            def _():
                remote(ps.at[l, b], xr.at[l, j - 1], xy_s.at[l], xy_r.at[l], dev(z, ny, nx, c)).start()

            return 0

        lax.fori_loop(1, NX * NY, send, 0)

    def mine(l):
        return xy - 2 * l

    def owner(l):
        return (mine(l) >= 0) & (mine(l) < OWN)

    def add_plane(l):
        @pl.when(owner(l))
        def _():
            wait_recv(xr.at[l], xy_s.at[l], xy_r.at[l])
            total = ps[l, mine(l)]
            for j in range(NX * NY - 1):
                total = total + xr[l, j]
            zs[l, z] = total

            def send(j, _):
                remote(zs.at[l, z], zs.at[l, z], zz_s.at[l], zz_r.at[l], dev((z + j) % NZ, y, x, c)).start()
                return 0

            lax.fori_loop(1, NZ, send, 0)

    def add_z(l):
        @pl.when(owner(l))
        def _():
            wait_recv(zs.at[l, pl.ds(0, NZ - 1)], zz_s.at[l], zz_r.at[l])
            total = zs[l, 0]
            for j in range(1, NZ):
                total = total + zs[l, j]
            b = c * OWN + mine(l)
            pf[l, b] = total

            def send(j, _):
                ny, nx = xy_peer(j)
                remote(pf.at[l, b], pf.at[l, b], ag_s.at[l], ag_r.at[l], dev(z, ny, nx, c)).start()
                return 0

            lax.fori_loop(1, NX * NY, send, 0)

    def share_core(l):
        @pl.when(owner(l))
        def _():
            wait_recv(pf.at[l, pl.ds(0, OWN - 1)], ag_s.at[l], ag_r.at[l])

        @pl.when(jnp.logical_not(owner(l)))
        def _():
            wait_recv(pf.at[l, pl.ds(0, OWN)], ag_s.at[l], ag_r.at[l])

        half = pf.at[l, pl.ds(c * OWN, OWN)]
        remote(half, half, ac_s.at[l], ac_r.at[l], partner).start()

    def grad(l, i0, i1):
        def step(i, _):
            rows = pl.ds(pl.multiple_of(i * GRAD_F, GRAD_F), GRAD_F)
            g = mm(s[l, :, rows], k[l], 0, 0) + e[l, rows, :].astype(F32)
            m[l, rows, :] = g
            top = g.astype(BF16)
            hi[l, rows, :] = top
            lo[l, rows, :] = (g - top.astype(F32)).astype(BF16)
            return 0

        lax.fori_loop(i0, i1, step, 0)

    def q_term(l):
        wait_recv(pf.at[l, pl.ds(0, OWN)], ac_s.at[l], ac_r.at[l])

        def step(i, acc):
            rows = pl.ds(pl.multiple_of(i * 512, 512), 512)
            p3 = split3(jnp.concatenate([pf[l, i * 4 + j] for j in range(4)], axis=1))
            r = fold3(mm(p3, hi[l, rows, :]))
            r2 = mm(p3[0 : 2 * RANK], lo[l, rows, :])
            return acc + (r + (r2[0:RANK] + r2[RANK : 2 * RANK]))

        u = lax.fori_loop(0, FEATS // 512, step, jnp.zeros((RANK, COLS), F32))
        for i in range(NY):
            ub[l, i] = u[8 * i : 8 * i + 8]

        def send(j, _):
            ny = (y + j) % NY
            remote(ub.at[l, ny], yr.at[l, j - 1], y1_s.at[l], y1_r.at[l], dev(z, ny, x, c)).start()
            return 0

        lax.fori_loop(1, NY, send, 0)

    def q_add_y(l):
        wait_recv(yr.at[l], y1_s.at[l], y1_r.at[l])
        zq[l, z] = ub[l, y] + yr[l, 0] + yr[l, 1] + yr[l, 2]

        def send(j, _):
            remote(zq.at[l, z], zq.at[l, z], qz_s.at[l], qz_r.at[l], dev((z + j) % NZ, y, x, c)).start()
            return 0

        lax.fori_loop(1, NZ, send, 0)

    def q_add_z(l):
        wait_recv(zq.at[l, pl.ds(0, NZ - 1)], qz_s.at[l], qz_r.at[l])
        total = zq[l, 0]
        for j in range(1, NZ):
            total = total + zq[l, j]
        qt[l, y] = total * (1.0 / (NZ * NY))

        def send(j, _):
            remote(qt.at[l, y], qt.at[l, y], y2_s.at[l], y2_r.at[l], dev(z, (y + j) % NY, x, c)).start()
            return 0

        lax.fori_loop(1, NY, send, 0)

    def gram(l):
        def step(i, acc):
            p3 = split3(jnp.concatenate([pf[l, i * 4 + j] for j in range(4)], axis=1))
            return acc + mm(p3, p3, 1, 1)

        g = lax.fori_loop(0, FEATS // 512, step, jnp.zeros((3 * RANK, 3 * RANK), F32))
        g = fold3(g)
        return g[:, 0:RANK] + g[:, RANK : 2 * RANK] + g[:, 2 * RANK : 3 * RANK]

    def inverse_factors(grams):
        rows = lax.broadcasted_iota(jnp.int32, (RANK, 1), 0)
        eye = (rows == lax.broadcasted_iota(jnp.int32, (RANK, RANK), 1)).astype(F32)
        work = [jnp.concatenate([g, eye], axis=1) for g in grams]
        for j in range(RANK):
            for n, a in enumerate(work):
                inv = lax.rsqrt(a[j : j + 1, j : j + 1])
                row = a[j : j + 1, :] * inv
                col = jnp.where(rows > j, a[:, j : j + 1] * inv, 0.0)
                work[n] = jnp.where(rows == j, row, a - col * row)
        return [a[:, RANK : 2 * RANK] for a in work]

    def ortho(l):
        def step(i, _):
            o = mm(gl[l], pf[l, i], precision=lax.Precision.HIGHEST)
            top = o.astype(BF16).astype(F32)
            rest = o - top
            wide = jnp.concatenate([top, top, rest, rest], axis=0)
            ot[l, pl.ds(pl.multiple_of(i * BLK, BLK), BLK), :] = wide.T.astype(BF16)
            return 0

        lax.fori_loop(0, NBLK, step, 0)

    def finish(l):
        wait_recv(qt.at[l, pl.ds(0, NY - 1)], y2_s.at[l], y2_r.at[l])
        u = jnp.concatenate([qt[l, i] for i in range(NY)], axis=0)
        q = mm(gl[l], u, precision=lax.Precision.HIGHEST)
        qo[l] = q
        top = q.astype(BF16)
        rest = (q - top.astype(F32)).astype(BF16)
        q4 = jnp.concatenate([top, rest, top, rest], axis=0)

        def step(i, _):
            rows = pl.ds(pl.multiple_of(i * 896, 896), 896)
            e[l, rows, :] = (m[l, rows, :] - mm(ot[l, rows, :], q4)).astype(BF16)
            return 0

        for part in range(2):
            lax.fori_loop(2 * part, 2 * part + 2, step, 0)
            rows = pl.ds(part * 1792, 1792)
            pltpu.make_async_copy(e.at[l, rows], err_hbm.at[0, l, rows], out_sem.at[2 * l + part]).start()

    p_term(0)
    add_cores(0)
    p_term(1)
    add_cores(1)
    cs[0][1].wait()
    grad(0, 0, 5)
    add_plane(0)
    grad(0, 5, 7)
    add_plane(1)
    cs[1][1].wait()
    grad(1, 0, 4)
    add_z(0)
    grad(1, 4, 7)
    add_z(1)
    share_core(0)
    q_term(0)
    g0 = gram(0)
    share_core(1)
    q_term(1)
    q_add_y(0)
    g1 = gram(1)
    q_add_y(1)
    inverses = inverse_factors([g0, g1])
    for l in range(LAYERS):
        gl[l] = inverses[l]
    q_add_z(0)
    ortho(0)
    q_add_z(1)
    ortho(1)
    finish(0)
    finish(1)
    out_q = pltpu.make_async_copy(qo, qf_hbm, out_sem.at[4])
    out_q.start()

    for l in range(LAYERS):
        wait_send(zl.at[l, 1], z_s.at[l], z_r.at[l])
        wait_send(cr.at[l], c_s.at[l], c_r.at[l])

        @pl.when(owner(l))
        def _():
            wait_send(ps.at[l, pl.ds(0, OWN - 1)], xy_s.at[l], xy_r.at[l])
            wait_send(zs.at[l, pl.ds(0, NZ - 1)], zz_s.at[l], zz_r.at[l])
            wait_send(pf.at[l, pl.ds(0, NX * NY - 1)], ag_s.at[l], ag_r.at[l])

        @pl.when(jnp.logical_not(owner(l)))
        def _():
            wait_send(ps.at[l, pl.ds(0, OWN)], xy_s.at[l], xy_r.at[l])

        wait_send(pf.at[l, pl.ds(0, OWN)], ac_s.at[l], ac_r.at[l])
        wait_send(ub.at[l, pl.ds(0, NY - 1)], y1_s.at[l], y1_r.at[l])
        wait_send(zq.at[l, pl.ds(0, NZ - 1)], qz_s.at[l], qz_r.at[l])
        wait_send(qt.at[l, pl.ds(0, NY - 1)], y2_s.at[l], y2_r.at[l])
        for part in range(2):
            rows = pl.ds(part * 1792, 1792)
            pltpu.make_async_copy(e.at[l, rows], err_hbm.at[0, l, rows], out_sem.at[2 * l + part]).wait()
    out_q.wait()


def body(saved_inputs, kv_cotangent, error_buffer, q_start):
    L = LAYERS
    pair = pltpu.SemaphoreType.DMA((L,))
    return pl.pallas_call(
        kernel,
        out_shape=(
            jax.ShapeDtypeStruct((1, L, FEATS, COLS), BF16),
            jax.ShapeDtypeStruct((L, RANK, COLS), F32),
        ),
        in_specs=[pl.BlockSpec(memory_space=pl.ANY)] * 4,
        out_specs=(pl.BlockSpec(memory_space=pl.ANY), pl.BlockSpec(memory_space=pl.ANY)),
        scratch_shapes=[
            pltpu.VMEM((L, TOK, FEATS), BF16),
            pltpu.VMEM((L, TOK, COLS), BF16),
            pltpu.VMEM((L, FEATS, COLS), BF16),
            pltpu.VMEM((L, RANK, COLS), F32),
            pltpu.VMEM((L, 3 * RANK, COLS), BF16),
            pltpu.VMEM((L, FEATS, COLS), F32),
            pltpu.VMEM((L, FEATS, COLS), BF16),
            pltpu.VMEM((L, FEATS, COLS), BF16),
            pltpu.VMEM((L, FEATS, 128), BF16),
            pltpu.VMEM((L, 2, RANK, HALF), F32),
            pltpu.VMEM((L, RANK, HALF), F32),
            pltpu.VMEM((L, 3 * RANK, HALF), BF16),
            pltpu.VMEM((L, NBLK, RANK, BLK), F32),
            pltpu.VMEM((L, OWN, RANK, BLK), F32),
            pltpu.VMEM((L, OWN, RANK, BLK), F32),
            pltpu.VMEM((L, NX * NY - 1, RANK, BLK), F32),
            pltpu.VMEM((L, NZ, RANK, BLK), F32),
            pltpu.VMEM((L, NBLK, RANK, BLK), F32),
            pltpu.VMEM((L, RANK, RANK), F32),
            pltpu.VMEM((L, NY, 8, COLS), F32),
            pltpu.VMEM((L, NY - 1, 8, COLS), F32),
            pltpu.VMEM((L, NZ, 8, COLS), F32),
            pltpu.VMEM((L, NY, 8, COLS), F32),
            pltpu.VMEM((L, RANK, COLS), F32),
            pltpu.SemaphoreType.DMA((11,)),
            pltpu.SemaphoreType.DMA((5,)),
        ]
        + [pair] * 18,
        compiler_params=pltpu.CompilerParams(
            collective_id=0, has_side_effects=True, vmem_limit_bytes=60 * 1024 * 1024
        ),
        cost_estimate=pl.CostEstimate(flops=8_600_000_000, bytes_accessed=39_000_000, transcendentals=0),
    )(saved_inputs, kv_cotangent, error_buffer, q_start)


def solution(mesh):
    placed = (
        P(None, "dp", None),
        P(None, "dp", "tensor"),
        P("dp", None, None, "tensor"),
        P(None, None, "tensor"),
    )
    return jax.shard_map(
        body,
        mesh=mesh,
        in_specs=placed,
        out_specs=(P("dp", None, None, "tensor"), P(None, None, "tensor")),
        check_vma=False,
    )
```

```python
import functools

import jax
import jax.numpy as jnp
from jax import lax
from jax.experimental import pallas as pl
from jax.experimental.pallas import tpu as pltpu
from jax.sharding import PartitionSpec as P

MESH = pl.DeviceIdType.MESH
F32, BF16 = jnp.float32, jnp.bfloat16
FEATS, RANK, LAYERS, TOK, COLS = 3584, 32, 2, 2048, 256
NZ, NY, NX = 8, 4, 4
HALF = TOK // 2
BLK = 128
NBLK = FEATS // BLK
OWN = NBLK // 2
GRAD_F = 512


def mm(a, b, ca=1, cb=0, precision=None):
    return lax.dot_general(a, b, (((ca,), (cb,)), ((), ())), precision=precision, preferred_element_type=F32)


def split3(v):
    hi = v.astype(BF16)
    rest = v - hi.astype(F32)
    mid = rest.astype(BF16)
    lo = (rest - mid.astype(F32)).astype(BF16)
    return jnp.concatenate([hi, mid, lo], axis=0)


def fold3(r):
    return r[0:RANK] + r[RANK : 2 * RANK] + r[2 * RANK : 3 * RANK]


def kernel(
    s_hbm, k_hbm, e_hbm, q_hbm, m, ot, gl, qt,
    s, k, e, qv, q3, hi, lo, zl, zr, z3, pp, cr, ps, xr, zs, pf, p3, ub, yr, zq,
    hs, z_s, z_r, c_s, c_r, xy_s, xy_r, zz_s, zz_r, ag_s, ag_r, ac_s, ac_r, y1_s, y1_r, qz_s, qz_r, y2_s, y2_r,
):
    dp, t = lax.axis_index("dp"), lax.axis_index("tensor")
    z, y, x, c = dp // NY, dp % NY, t // 2, t % 2
    xy = y * NX + x

    def dev(z_, y_, x_, c_):
        return (z_ * NY + y_, x_ * 2 + c_)

    partner = dev(z, y, x, 1 - c)

    def xy_peer(j):
        return (y + j // NX) % NY, (x + j % NX) % NX

    def remote(src, dst, ss, rs, device):
        return pltpu.make_async_remote_copy(
            src_ref=src, dst_ref=dst, send_sem=ss, recv_sem=rs, device_id=device, device_id_type=MESH
        )

    def wait_recv(ref, ss, rs):
        remote(ref, ref, ss, rs, partner).wait_recv()

    def wait_send(ref, ss, rs):
        remote(ref, ref, ss, rs, partner).wait_send()

    barrier = pltpu.get_barrier_semaphore()
    pl.semaphore_signal(barrier, inc=1, device_id=partner, device_id_type=MESH)

    def greet_z(j, _):
        pl.semaphore_signal(barrier, inc=1, device_id=dev((z + j) % NZ, y, x, c), device_id_type=MESH)
        return 0

    def greet_xy(j, _):
        ny, nx = xy_peer(j)
        pl.semaphore_signal(barrier, inc=1, device_id=dev(z, ny, nx, c), device_id_type=MESH)
        return 0

    lax.fori_loop(1, NZ, greet_z, 0)
    lax.fori_loop(1, NX * NY, greet_xy, 0)

    def token_copy(hbm, vmem, l, part, first, count, sem):
        rows = pl.ds(pl.multiple_of((c if part == 0 else 1 - c) * HALF + first, count), count)
        return pltpu.make_async_copy(hbm.at[l, rows], vmem.at[l, pl.ds(part * HALF + first, count)], sem)

    cq = pltpu.make_async_copy(q_hbm, qv, hs.at[0])
    ck = [[token_copy(k_hbm, k, l, h, 0, HALF, hs.at[1 + 2 * l + h]) for h in range(2)] for l in range(LAYERS)]
    ce = [pltpu.make_async_copy(e_hbm.at[0, l], e.at[l], hs.at[5 + l]) for l in range(LAYERS)]
    own = [
        [token_copy(s_hbm, s, l, 0, i * HALF // 2, HALF // 2, hs.at[7 + 2 * l + i]) for i in range(2)] for l in range(LAYERS)
    ]
    rest = [token_copy(s_hbm, s, l, 1, 0, HALF, hs.at[11 + l]) for l in range(LAYERS)]
    cq.start()
    for l in range(LAYERS):
        ck[l][0].start()
        ck[l][1].start()
    ce[0].start()
    ce[1].start()

    cq.wait()
    for l in range(LAYERS):
        q3[l] = split3(qv[l])
    for l in range(LAYERS):
        ck[l][0].wait()
        ck[l][1].wait()
        own[0][l].start()
        for h in range(2):
            zl[l, h] = fold3(mm(q3[l], k[l, pl.ds(h * HALF, HALF), :], 1, 1))

    def error_part(l):
        ce[l].wait()
        for i in range(4):
            r = fold3(mm(q3[l], e[l, pl.ds(i * 896, 896), :], 1, 1))
            for j in range(7):
                pp[l, i * 7 + j] = r[:, j * BLK : (j + 1) * BLK]

    error_part(0)
    own[1][0].start()
    error_part(1)

    pl.semaphore_wait(barrier, 1 + (NZ - 1) + (NX * NY - 1))
    for l in range(LAYERS):
        remote(zl.at[l, 1], zr.at[l], z_s.at[l], z_r.at[l], partner).start()

    def p_blocks(l, side):
        for i in range(2):
            b0 = side * OWN + i * 7
            f0 = pl.multiple_of(b0 * BLK, BLK)
            r = fold3(mm(z3[l], s[l, pl.ds(0, HALF), pl.ds(f0, 7 * BLK)]))
            for j in range(7):
                pp[l, b0 + j] += r[:, j * BLK : (j + 1) * BLK]

    def p_term(l):
        wait_recv(zr.at[l], z_s.at[l], z_r.at[l])
        z3[l] = split3(zl[l, 0] + zr[l])
        own[l][0].wait()
        if l == 0:
            own[1][1].start()
        else:
            rest[0].start()
        own[l][1].wait()
        if l == 1:
            rest[1].start()
        p_blocks(l, 1 - c)
        remote(pp.at[l, pl.ds((1 - c) * OWN, OWN)], cr.at[l], c_s.at[l], c_r.at[l], partner).start()
        p_blocks(l, c)

    def add_cores(l):
        wait_recv(cr.at[l], c_s.at[l], c_r.at[l])

        def step(b, _):
            ps[l, b] = pp[l, c * OWN + b] + cr[l, b]
            return 0

        lax.fori_loop(0, OWN, step, 0)

        def send(j, _):
            ny, nx = xy_peer(j)
            b = ny * NX + nx - 2 * l

            @pl.when((b >= 0) & (b < OWN))
            def _():
                remote(ps.at[l, b], xr.at[l, j - 1], xy_s.at[l], xy_r.at[l], dev(z, ny, nx, c)).start()

            return 0

        lax.fori_loop(1, NX * NY, send, 0)

    def mine(l):
        return xy - 2 * l

    def owner(l):
        return (mine(l) >= 0) & (mine(l) < OWN)

    def add_plane(l):
        @pl.when(owner(l))
        def _():
            wait_recv(xr.at[l], xy_s.at[l], xy_r.at[l])
            total = ps[l, mine(l)]
            for j in range(NX * NY - 1):
                total = total + xr[l, j]
            zs[l, z] = total

            def send(j, _):
                remote(zs.at[l, z], zs.at[l, z], zz_s.at[l], zz_r.at[l], dev((z + j) % NZ, y, x, c)).start()
                return 0

            lax.fori_loop(1, NZ, send, 0)

    def add_z(l):
        @pl.when(owner(l))
        def _():
            wait_recv(zs.at[l, pl.ds(0, NZ - 1)], zz_s.at[l], zz_r.at[l])
            total = zs[l, 0]
            for j in range(1, NZ):
                total = total + zs[l, j]
            b = c * OWN + mine(l)
            pf[l, b] = total

            def send(j, _):
                ny, nx = xy_peer(j)
                remote(pf.at[l, b], pf.at[l, b], ag_s.at[l], ag_r.at[l], dev(z, ny, nx, c)).start()
                return 0

            lax.fori_loop(1, NX * NY, send, 0)

    def share_core(l):
        @pl.when(owner(l))
        def _():
            wait_recv(pf.at[l, pl.ds(0, OWN - 1)], ag_s.at[l], ag_r.at[l])

        @pl.when(jnp.logical_not(owner(l)))
        def _():
            wait_recv(pf.at[l, pl.ds(0, OWN)], ag_s.at[l], ag_r.at[l])

        half = pf.at[l, pl.ds(c * OWN, OWN)]
        remote(half, half, ac_s.at[l], ac_r.at[l], partner).start()

    def grad(l, i0, i1):
        for i in range(i0, i1):
            rows = pl.ds(i * GRAD_F, GRAD_F)
            g = mm(s[l, :, rows], k[l], 0, 0) + e[l, rows, :].astype(F32)
            m[l, rows, :] = g
            top = g.astype(BF16)
            hi[l, rows, :] = top
            lo[l, rows, :] = (g - top.astype(F32)).astype(BF16)

    def q_term(l):
        wait_recv(pf.at[l, pl.ds(0, OWN)], ac_s.at[l], ac_r.at[l])
        u = jnp.zeros((RANK, COLS), F32)
        for i in range(FEATS // 512):
            rows = pl.ds(i * 512, 512)
            terms = split3(jnp.concatenate([pf[l, i * 4 + j] for j in range(4)], axis=1))
            p3[l, :, rows] = terms
            r = fold3(mm(terms, hi[l, rows, :]))
            r2 = mm(terms[0 : 2 * RANK], lo[l, rows, :])
            u = u + (r + (r2[0:RANK] + r2[RANK : 2 * RANK]))
        for i in range(NY):
            ub[l, i] = u[8 * i : 8 * i + 8]

        def send(j, _):
            ny = (y + j) % NY
            remote(ub.at[l, ny], yr.at[l, j - 1], y1_s.at[l], y1_r.at[l], dev(z, ny, x, c)).start()
            return 0

        lax.fori_loop(1, NY, send, 0)

    def q_add_y(l):
        wait_recv(yr.at[l], y1_s.at[l], y1_r.at[l])
        zq[l, z] = ub[l, y] + yr[l, 0] + yr[l, 1] + yr[l, 2]

        def send(j, _):
            remote(zq.at[l, z], zq.at[l, z], qz_s.at[l], qz_r.at[l], dev((z + j) % NZ, y, x, c)).start()
            return 0

        lax.fori_loop(1, NZ, send, 0)

    def q_add_z(l):
        wait_recv(zq.at[l, pl.ds(0, NZ - 1)], qz_s.at[l], qz_r.at[l])
        total = zq[l, 0]
        for j in range(1, NZ):
            total = total + zq[l, j]
        qt[l, y] = total * (1.0 / (NZ * NY))

        def send(j, _):
            remote(qt.at[l, y], qt.at[l, y], y2_s.at[l], y2_r.at[l], dev(z, (y + j) % NY, x, c)).start()
            return 0

        lax.fori_loop(1, NY, send, 0)

    def gram(l):
        g = jnp.zeros((3 * RANK, 3 * RANK), F32)
        for i in range(FEATS // 512):
            terms = p3[l, :, pl.ds(i * 512, 512)]
            g = g + mm(terms, terms, 1, 1)
        g = fold3(g)
        return g[:, 0:RANK] + g[:, RANK : 2 * RANK] + g[:, 2 * RANK : 3 * RANK]

    def inverse_factors(grams):
        rows = lax.broadcasted_iota(jnp.int32, (RANK, 1), 0)
        eye = (rows == lax.broadcasted_iota(jnp.int32, (RANK, RANK), 1)).astype(F32)
        work = [jnp.concatenate([g, eye], axis=1) for g in grams]
        for j in range(RANK):
            for n, a in enumerate(work):
                inv = lax.rsqrt(a[j : j + 1, j : j + 1])
                row = a[j : j + 1, :] * inv
                col = jnp.where(rows > j, a[:, j : j + 1] * inv, 0.0)
                work[n] = jnp.where(rows == j, row, a - col * row)
        return [a[:, RANK : 2 * RANK] for a in work]

    def ortho(l):
        g3 = split3(gl[l])
        top, mid, low = g3[0:RANK], g3[RANK : 2 * RANK], g3[2 * RANK : 3 * RANK]
        left = jnp.concatenate([top, top, top, mid, mid, low], axis=1)
        for i in range(FEATS // 512):
            rows = pl.ds(i * 512, 512)
            p_top, p_mid, p_low = (p3[l, pl.ds(n * RANK, RANK), rows] for n in range(3))
            o = mm(left, jnp.concatenate([p_top, p_mid, p_low, p_top, p_mid, p_top], axis=0))
            o_top = o.astype(BF16)
            o_low = (o - o_top.astype(F32)).astype(BF16)
            ot[l, rows, :] = jnp.concatenate([o_top, o_top, o_low, o_low], axis=0).T

    p_term(0)
    add_cores(0)
    p_term(1)
    add_cores(1)
    rest[0].wait()
    grad(0, 0, 4)
    add_plane(0)
    grad(0, 4, 7)
    add_plane(1)
    rest[1].wait()
    grad(1, 0, 4)
    add_z(0)
    grad(1, 4, 7)
    add_z(1)
    share_core(0)
    q_term(0)
    g0 = gram(0)
    share_core(1)
    q_term(1)
    q_add_y(0)
    g1 = gram(1)
    q_add_y(1)
    inverses = inverse_factors([g0, g1])
    for l in range(LAYERS):
        gl[l] = inverses[l]
    q_add_z(0)
    ortho(0)
    q_add_z(1)
    ortho(1)
    for l in range(LAYERS):
        wait_recv(qt.at[l, pl.ds(0, NY - 1)], y2_s.at[l], y2_r.at[l])

    for l in range(LAYERS):
        wait_send(zl.at[l, 1], z_s.at[l], z_r.at[l])
        wait_send(cr.at[l], c_s.at[l], c_r.at[l])

        @pl.when(owner(l))
        def _():
            wait_send(ps.at[l, pl.ds(0, OWN - 1)], xy_s.at[l], xy_r.at[l])
            wait_send(zs.at[l, pl.ds(0, NZ - 1)], zz_s.at[l], zz_r.at[l])
            wait_send(pf.at[l, pl.ds(0, NX * NY - 1)], ag_s.at[l], ag_r.at[l])

        @pl.when(jnp.logical_not(owner(l)))
        def _():
            wait_send(ps.at[l, pl.ds(0, OWN)], xy_s.at[l], xy_r.at[l])

        wait_send(pf.at[l, pl.ds(0, OWN)], ac_s.at[l], ac_r.at[l])
        wait_send(ub.at[l, pl.ds(0, NY - 1)], y1_s.at[l], y1_r.at[l])
        wait_send(zq.at[l, pl.ds(0, NZ - 1)], qz_s.at[l], qz_r.at[l])
        wait_send(qt.at[l, pl.ds(0, NY - 1)], y2_s.at[l], y2_r.at[l])


def finish(m, ot, gl, qt, err_hbm, qf, out, sems):
    copies = []
    for l in range(LAYERS):
        u = jnp.concatenate([qt[l, i] for i in range(NY)], axis=0)
        q = mm(gl[l], u, precision=lax.Precision.HIGHEST)
        qf[l] = q
        top = q.astype(BF16)
        rest = (q - top.astype(F32)).astype(BF16)
        q4 = jnp.concatenate([top, rest, top, rest], axis=0)
        for i in range(FEATS // 512):
            rows = pl.ds(i * 512, 512)
            out[l, rows, :] = (m[l, rows, :] - mm(ot[l, rows, :], q4)).astype(BF16)
            copies.append(pltpu.make_async_copy(out.at[l, rows], err_hbm.at[0, l, rows], sems.at[len(copies)]))
            copies[-1].start()
    for copy in copies:
        copy.wait()


def body(saved_inputs, kv_cotangent, error_buffer, q_start):
    L = LAYERS
    pair = pltpu.SemaphoreType.DMA((L,))
    any_spec, vmem_spec = pl.BlockSpec(memory_space=pl.ANY), pl.BlockSpec(memory_space=pltpu.VMEM)
    held = pl.pallas_call(
        kernel,
        out_shape=(
            pltpu.VMEM((L, FEATS, COLS), F32),
            pltpu.VMEM((L, FEATS, 128), BF16),
            pltpu.VMEM((L, RANK, RANK), F32),
            pltpu.VMEM((L, NY, 8, COLS), F32),
        ),
        in_specs=[any_spec] * 4,
        out_specs=(vmem_spec,) * 4,
        scratch_shapes=[
            pltpu.VMEM((L, TOK, FEATS), BF16),
            pltpu.VMEM((L, TOK, COLS), BF16),
            pltpu.VMEM((L, FEATS, COLS), BF16),
            pltpu.VMEM((L, RANK, COLS), F32),
            pltpu.VMEM((L, 3 * RANK, COLS), BF16),
            pltpu.VMEM((L, FEATS, COLS), BF16),
            pltpu.VMEM((L, FEATS, COLS), BF16),
            pltpu.VMEM((L, 2, RANK, HALF), F32),
            pltpu.VMEM((L, RANK, HALF), F32),
            pltpu.VMEM((L, 3 * RANK, HALF), BF16),
            pltpu.VMEM((L, NBLK, RANK, BLK), F32),
            pltpu.VMEM((L, OWN, RANK, BLK), F32),
            pltpu.VMEM((L, OWN, RANK, BLK), F32),
            pltpu.VMEM((L, NX * NY - 1, RANK, BLK), F32),
            pltpu.VMEM((L, NZ, RANK, BLK), F32),
            pltpu.VMEM((L, NBLK, RANK, BLK), F32),
            pltpu.VMEM((L, 3 * RANK, FEATS), BF16),
            pltpu.VMEM((L, NY, 8, COLS), F32),
            pltpu.VMEM((L, NY - 1, 8, COLS), F32),
            pltpu.VMEM((L, NZ, 8, COLS), F32),
            pltpu.SemaphoreType.DMA((13,)),
        ]
        + [pair] * 18,
        compiler_params=pltpu.CompilerParams(
            collective_id=0, has_side_effects=True, vmem_limit_bytes=50 * 1024 * 1024
        ),
        cost_estimate=pl.CostEstimate(flops=8_400_000_000, bytes_accessed=35_000_000, transcendentals=0),
    )(saved_inputs, kv_cotangent, error_buffer, q_start)
    return pl.pallas_call(
        finish,
        out_shape=(
            jax.ShapeDtypeStruct((1, L, FEATS, COLS), BF16),
            jax.ShapeDtypeStruct((L, RANK, COLS), F32),
        ),
        in_specs=[vmem_spec] * 4,
        out_specs=(any_spec, vmem_spec),
        scratch_shapes=[pltpu.VMEM((L, FEATS, COLS), BF16), pltpu.SemaphoreType.DMA((2 * FEATS // 512,))],
        compiler_params=pltpu.CompilerParams(vmem_limit_bytes=16 * 1024 * 1024),
        cost_estimate=pl.CostEstimate(flops=240_000_000, bytes_accessed=4_000_000, transcendentals=0),
    )(*(pltpu.with_memory_space_constraint(a, pltpu.VMEM) for a in held))


def solution(mesh):
    placed = (
        P(None, "dp", None),
        P(None, "dp", "tensor"),
        P("dp", None, None, "tensor"),
        P(None, None, "tensor"),
    )
    return jax.shard_map(
        body,
        mesh=mesh,
        in_specs=placed,
        out_specs=(P("dp", None, None, "tensor"), P(None, None, "tensor")),
        check_vma=False,
    )
```

```python
import functools

import jax
import jax.numpy as jnp
from jax import lax
from jax.experimental import pallas as pl
from jax.experimental.pallas import tpu as pltpu
from jax.sharding import PartitionSpec as P

MESH = pl.DeviceIdType.MESH
F32, BF16 = jnp.float32, jnp.bfloat16
FEATS, RANK, LAYERS, TOK, COLS = 3584, 32, 2, 2048, 256
NZ, NY, NX = 8, 4, 4
HALF = TOK // 2
BLK = 128
NBLK = FEATS // BLK
OWN = NBLK // 2
GRAD_F = 512


def mm(a, b, ca=1, cb=0):
    return lax.dot_general(a, b, (((ca,), (cb,)), ((), ())), preferred_element_type=F32)


def split3(v):
    hi = v.astype(BF16)
    rest = v - hi.astype(F32)
    mid = rest.astype(BF16)
    lo = (rest - mid.astype(F32)).astype(BF16)
    return jnp.concatenate([hi, mid, lo], axis=0)


def fold3(r):
    return r[0:RANK] + r[RANK : 2 * RANK] + r[2 * RANK : 3 * RANK]


SUB = 1
ROWS = RANK // SUB
CUT = 3 * GRAD_F
XY_ORDER = sorted(range(1, NX * NY), key=lambda j: -(min(j % NX, NX - j % NX) + min(j // NX, NY - j // NX)))
Z_ORDER = sorted(range(1, NZ), key=lambda j: -min(j, NZ - j))
Y_ORDER = (2, 1, 3)


def new_error(m, ot, q, rows):
    top = q.astype(BF16)
    rest = (q - top.astype(F32)).astype(BF16)
    return (m[rows, :] - mm(ot[rows, :], jnp.concatenate([top, rest, top, rest], axis=0))).astype(BF16)


def wide_left(v):
    t = split3(v)
    top, mid, low = t[0:RANK], t[RANK : 2 * RANK], t[2 * RANK : 3 * RANK]
    return jnp.concatenate([top, top, top, mid, mid, low], axis=1)


def right_of(top, mid, low):
    return jnp.concatenate([top, mid, low, top, mid, top], axis=0)


def q_from(gl, qt):
    t = split3(jnp.concatenate([qt[i] for i in range(NY)], axis=0))
    return mm(gl[...], right_of(t[0:RANK], t[RANK : 2 * RANK], t[2 * RANK : 3 * RANK]))


def kernel(
    s_hbm, k_hbm, e_hbm, q_hbm, err0, q0, m1, ot1, gl1, qt1,
    s, k, e1, qv, q3, m0, ot0, gl0, qt0, hi, lo, zl, zr, z3, pp, cr, ps, xr, zs, pf, p3, ub, yr, zq,
    hs, z_s, z_r, c_s, c_r, xy_s, xy_r, zz_s, zz_r, ag_s, ag_r, ac_s, ac_r, y1_s, y1_r, qz_s, qz_r, y2_s, y2_r,
):
    e, m, ot, gl, qt = (err0, e1), (m0, m1), (ot0, ot1), (gl0, gl1), (qt0, qt1)
    dp, t = lax.axis_index("dp"), lax.axis_index("tensor")
    z, y, x, c = dp // NY, dp % NY, t // 2, t % 2
    xy = y * NX + x

    def dev(z_, y_, x_, c_):
        return (z_ * NY + y_, x_ * 2 + c_)

    partner = dev(z, y, x, 1 - c)

    def xy_peer(j):
        return (y + j // NX) % NY, (x + j % NX) % NX

    def remote(src, dst, ss, rs, device):
        return pltpu.make_async_remote_copy(
            src_ref=src, dst_ref=dst, send_sem=ss, recv_sem=rs, device_id=device, device_id_type=MESH
        )

    def wait_recv(ref, ss, rs):
        remote(ref, ref, ss, rs, partner).wait_recv()

    def wait_send(ref, ss, rs):
        remote(ref, ref, ss, rs, partner).wait_send()

    barrier = pltpu.get_barrier_semaphore()
    pl.semaphore_signal(barrier, inc=1, device_id=partner, device_id_type=MESH)

    def greet_z(j, _):
        pl.semaphore_signal(barrier, inc=1, device_id=dev((z + j) % NZ, y, x, c), device_id_type=MESH)
        return 0

    def greet_xy(j, _):
        ny, nx = xy_peer(j)
        pl.semaphore_signal(barrier, inc=1, device_id=dev(z, ny, nx, c), device_id_type=MESH)
        return 0

    lax.fori_loop(1, NZ, greet_z, 0)
    lax.fori_loop(1, NX * NY, greet_xy, 0)

    def token_copy(hbm, vmem, l, part, cols, sem):
        rows = pl.ds(pl.multiple_of((c if part == 0 else 1 - c) * HALF, HALF), HALF)
        return pltpu.make_async_copy(hbm.at[l, rows, cols], vmem.at[l, pl.ds(part * HALF, HALF), cols], sem)

    def side_cols(side):
        return pl.ds(pl.multiple_of(side * (FEATS // 2), FEATS // 2), FEATS // 2)

    cq = pltpu.make_async_copy(q_hbm, qv, hs.at[0])
    ck = [[token_copy(k_hbm, k, l, h, pl.ds(0, COLS), hs.at[1 + 2 * l + h]) for h in range(2)] for l in range(LAYERS)]
    ce = [pltpu.make_async_copy(e_hbm.at[0, l], e[l], hs.at[5 + l]) for l in range(LAYERS)]
    own = [
        [token_copy(s_hbm, s, l, 0, side_cols(side), hs.at[7 + 2 * l + i]) for i, side in enumerate((1 - c, c))]
        for l in range(LAYERS)
    ]
    rest = [
        [token_copy(s_hbm, s, l, 1, cols, hs.at[11 + 2 * l + i]) for i, cols in enumerate((pl.ds(0, CUT), pl.ds(CUT, FEATS - CUT)))]
        for l in range(LAYERS)
    ]
    cq.start()
    for l in range(LAYERS):
        ck[l][0].start()
        ck[l][1].start()
    ce[0].start()
    ce[1].start()

    cq.wait()
    for l in range(LAYERS):
        q3[l] = split3(qv[l])
    for l in range(LAYERS):
        ck[l][0].wait()
        ck[l][1].wait()
        own[0][l].start()
        for h in range(2):
            zl[l, h] = fold3(mm(q3[l], k[l, pl.ds(h * HALF, HALF), :], 1, 1))

    def error_part(l):
        ce[l].wait()
        for i in range(4):
            r = fold3(mm(q3[l], e[l][pl.ds(i * 896, 896), :], 1, 1))
            for h in range(SUB):
                for j in range(7):
                    pp[l, h, i * 7 + j] = r[h * ROWS : (h + 1) * ROWS, j * BLK : (j + 1) * BLK]

    error_part(0)
    own[1][0].start()
    error_part(1)

    pl.semaphore_wait(barrier, 1 + (NZ - 1) + (NX * NY - 1))
    for l in range(LAYERS):
        remote(zl.at[l, 1], zr.at[l], z_s.at[l], z_r.at[l], partner).start()

    def p_blocks(l, side):
        for i in range(2):
            b0 = side * OWN + i * 7
            f0 = pl.multiple_of(b0 * BLK, BLK)
            r = fold3(mm(z3[l], s[l, pl.ds(0, HALF), pl.ds(f0, 7 * BLK)]))
            for h in range(SUB):
                for j in range(7):
                    pp[l, h, b0 + j] += r[h * ROWS : (h + 1) * ROWS, j * BLK : (j + 1) * BLK]

    def p_other(l):
        wait_recv(zr.at[l], z_s.at[l], z_r.at[l])
        z3[l] = split3(zl[l, 0] + zr[l])
        own[l][0].wait()
        if l == 0:
            own[1][1].start()
        else:
            rest[0][1].start()
        p_blocks(l, 1 - c)
        for h in range(SUB):
            remote(pp.at[l, h, pl.ds((1 - c) * OWN, OWN)], cr.at[l, h], c_s.at[l, h], c_r.at[l, h], partner).start()

    def p_mine(l):
        own[l][1].wait()
        if l == 0:
            rest[0][0].start()
        else:
            rest[1][0].start()
            rest[1][1].start()
        p_blocks(l, c)

    def mine(l):
        return xy - 2 * l

    def owner(l):
        return (mine(l) >= 0) & (mine(l) < OWN)

    def add_cores(l, h):
        wait_recv(cr.at[l, h], c_s.at[l, h], c_r.at[l, h])
        for b in range(OWN):
            ps[l, h, b] = pp[l, h, c * OWN + b] + cr[l, h, b]
        for j in XY_ORDER:
            ny, nx = xy_peer(j)
            b = ny * NX + nx - 2 * l

            @pl.when((b >= 0) & (b < OWN))
            def _():
                remote(ps.at[l, h, b], xr.at[l, h, j - 1], xy_s.at[l, h], xy_r.at[l, h], dev(z, ny, nx, c)).start()

    def add_plane(l, h):
        @pl.when(owner(l))
        def _():
            wait_recv(xr.at[l, h], xy_s.at[l, h], xy_r.at[l, h])
            total = ps[l, h, mine(l)]
            for j in range(NX * NY - 1):
                total = total + xr[l, h, j]
            zs[l, h, z] = total
            for j in Z_ORDER:
                there = dev((z + j) % NZ, y, x, c)
                remote(zs.at[l, h, z], zs.at[l, h, z], zz_s.at[l, h], zz_r.at[l, h], there).start()

    def add_z(l, h):
        @pl.when(owner(l))
        def _():
            wait_recv(zs.at[l, h, pl.ds(0, NZ - 1)], zz_s.at[l, h], zz_r.at[l, h])
            total = zs[l, h, 0]
            for j in range(1, NZ):
                total = total + zs[l, h, j]
            b = c * OWN + mine(l)
            pf[l, h, b] = total
            for j in XY_ORDER:
                ny, nx = xy_peer(j)
                remote(pf.at[l, h, b], pf.at[l, h, b], ag_s.at[l, h], ag_r.at[l, h], dev(z, ny, nx, c)).start()

    def share_core(l, h):
        @pl.when(owner(l))
        def _():
            wait_recv(pf.at[l, h, pl.ds(0, OWN - 1)], ag_s.at[l, h], ag_r.at[l, h])

        @pl.when(jnp.logical_not(owner(l)))
        def _():
            wait_recv(pf.at[l, h, pl.ds(0, OWN)], ag_s.at[l, h], ag_r.at[l, h])

        half = pf.at[l, h, pl.ds(c * OWN, OWN)]
        remote(half, half, ac_s.at[l, h], ac_r.at[l, h], partner).start()

    def grad(l, i0, i1):
        for i in range(i0, i1):
            rows = pl.ds(i * GRAD_F, GRAD_F)
            if i == 0 or i * GRAD_F == CUT:
                rest[l][0 if i == 0 else 1].wait()
            g = mm(s[l, :, rows], k[l], 0, 0) + e[l][rows, :].astype(F32)
            m[l][rows, :] = g
            top = g.astype(BF16)
            hi[l, rows, :] = top
            lo[l, rows, :] = (g - top.astype(F32)).astype(BF16)

    def q_half(l, side):
        u = jnp.zeros((RANK, COLS), F32)
        for i in range(OWN // 2):
            b0 = side * OWN + 2 * i
            rows = pl.ds(pl.multiple_of(b0 * BLK, 2 * BLK), 2 * BLK)
            halves = [jnp.concatenate([pf[l, h, b0], pf[l, h, b0 + 1]], axis=1) for h in range(SUB)]
            terms = split3(jnp.concatenate(halves, axis=0))
            p3[l, :, rows] = terms
            r = fold3(mm(terms, hi[l, rows, :]))
            r2 = mm(terms[0 : 2 * RANK], lo[l, rows, :])
            u = u + (r + (r2[0:RANK] + r2[RANK : 2 * RANK]))
        return u

    def q_send(l, u):
        for i in range(NY):
            ub[l, i] = u[8 * i : 8 * i + 8]

        for j in Y_ORDER:
            ny = (y + j) % NY
            remote(ub.at[l, ny], yr.at[l, j - 1], y1_s.at[l], y1_r.at[l], dev(z, ny, x, c)).start()

    def q_add_y(l):
        wait_recv(yr.at[l], y1_s.at[l], y1_r.at[l])
        zq[l, z] = ub[l, y] + yr[l, 0] + yr[l, 1] + yr[l, 2]
        for j in Z_ORDER:
            remote(zq.at[l, z], zq.at[l, z], qz_s.at[l], qz_r.at[l], dev((z + j) % NZ, y, x, c)).start()

    def q_add_z(l):
        wait_recv(zq.at[l, pl.ds(0, NZ - 1)], qz_s.at[l], qz_r.at[l])
        total = zq[l, 0]
        for j in range(1, NZ):
            total = total + zq[l, j]
        qt[l][y] = total * (1.0 / (NZ * NY))
        for j in Y_ORDER:
            remote(qt[l].at[y], qt[l].at[y], y2_s.at[l], y2_r.at[l], dev(z, (y + j) % NY, x, c)).start()

    def gram(l):
        g = jnp.zeros((3 * RANK, 3 * RANK), F32)
        for i in range(FEATS // 512):
            terms = p3[l, :, pl.ds(i * 512, 512)]
            g = g + mm(terms, terms, 1, 1)
        g = fold3(g)
        return g[:, 0:RANK] + g[:, RANK : 2 * RANK] + g[:, 2 * RANK : 3 * RANK]

    def inverse_factors(grams):
        rows = lax.broadcasted_iota(jnp.int32, (RANK, 1), 0)
        eye = (rows == lax.broadcasted_iota(jnp.int32, (RANK, RANK), 1)).astype(F32)
        work = [jnp.concatenate([g, eye], axis=1) for g in grams]
        for j in range(RANK):
            for n, a in enumerate(work):
                inv = lax.rsqrt(a[j : j + 1, j : j + 1])
                row = a[j : j + 1, :] * inv
                col = jnp.where(rows > j, a[:, j : j + 1] * inv, 0.0)
                work[n] = jnp.where(rows == j, row, a - col * row)
        return [a[:, RANK : 2 * RANK] for a in work]

    def ortho(l):
        for i in range(FEATS // 512):
            rows = pl.ds(i * 512, 512)
            o = mm(gl[l][...], right_of(*(p3[l, pl.ds(n * RANK, RANK), rows] for n in range(3))))
            o_top = o.astype(BF16)
            o_low = (o - o_top.astype(F32)).astype(BF16)
            ot[l][rows, :] = jnp.concatenate([o_top, o_top, o_low, o_low], axis=0).T

    pairs = [(l, h) for l in range(LAYERS) for h in range(SUB)]
    for l in range(LAYERS):
        p_other(l)
        p_mine(l)
        for h in range(SUB):
            add_cores(l, h)
    grad(0, 0, 5)
    for l, h in pairs:
        add_plane(l, h)
    grad(0, 5, 7)
    grad(1, 0, 3)
    for l, h in pairs:
        add_z(l, h)
    grad(1, 3, 7)
    for l, h in pairs:
        share_core(l, h)
    own_q = [q_half(l, c) for l in range(LAYERS)]
    for l in range(LAYERS):
        for h in range(SUB):
            wait_recv(pf.at[l, h, pl.ds(0, OWN)], ac_s.at[l, h], ac_r.at[l, h])
        q_send(l, own_q[l] + q_half(l, 1 - c))
    grams = [gram(l) for l in range(LAYERS)]
    for l in range(LAYERS):
        q_add_y(l)
    for l, inverse in enumerate(inverse_factors(grams)):
        gl[l][...] = wide_left(inverse)
    for l in range(LAYERS):
        q_add_z(l)
    ortho(0)
    ortho(1)
    wait_recv(qt[0].at[pl.ds(0, NY - 1)], y2_s.at[0], y2_r.at[0])
    q0[...] = q_from(gl[0], qt[0])
    for i in range(FEATS // 512):
        rows = pl.ds(i * 512, 512)
        err0[rows, :] = new_error(m[0], ot[0], q0[...], rows)
    wait_recv(qt[1].at[pl.ds(0, NY - 1)], y2_s.at[1], y2_r.at[1])

    for l in range(LAYERS):
        wait_send(zl.at[l, 1], z_s.at[l], z_r.at[l])
        for h in range(SUB):
            wait_send(cr.at[l, h], c_s.at[l, h], c_r.at[l, h])

            @pl.when(owner(l))
            def _():
                wait_send(ps.at[l, h, pl.ds(0, OWN - 1)], xy_s.at[l, h], xy_r.at[l, h])
                wait_send(zs.at[l, h, pl.ds(0, NZ - 1)], zz_s.at[l, h], zz_r.at[l, h])
                wait_send(pf.at[l, h, pl.ds(0, NX * NY - 1)], ag_s.at[l, h], ag_r.at[l, h])

            @pl.when(jnp.logical_not(owner(l)))
            def _():
                wait_send(ps.at[l, h, pl.ds(0, OWN)], xy_s.at[l, h], xy_r.at[l, h])

            wait_send(pf.at[l, h, pl.ds(0, OWN)], ac_s.at[l, h], ac_r.at[l, h])
        wait_send(ub.at[l, pl.ds(0, NY - 1)], y1_s.at[l], y1_r.at[l])
        wait_send(zq.at[l, pl.ds(0, NZ - 1)], qz_s.at[l], qz_r.at[l])
        wait_send(qt[l].at[pl.ds(0, NY - 1)], y2_s.at[l], y2_r.at[l])


def finish(err0, q0, m1, ot1, gl1, qt1, err_hbm, qf, out, sems):
    first = pltpu.make_async_copy(err0, err_hbm.at[0, 0], sems.at[0])
    first.start()
    copies = [first]
    q = q_from(gl1, qt1)
    qf[0] = q0[...]
    qf[1] = q
    for i in range(FEATS // 512):
        rows = pl.ds(i * 512, 512)
        out[rows, :] = new_error(m1, ot1, q, rows)
        copies.append(pltpu.make_async_copy(out.at[rows], err_hbm.at[0, 1, rows], sems.at[1 + i]))
        copies[-1].start()
    for copy in copies:
        copy.wait()


def body(saved_inputs, kv_cotangent, error_buffer, q_start):
    L = LAYERS
    pair, four = pltpu.SemaphoreType.DMA((L,)), pltpu.SemaphoreType.DMA((L, SUB))
    any_spec, vmem_spec = pl.BlockSpec(memory_space=pl.ANY), pl.BlockSpec(memory_space=pltpu.VMEM)
    held = pl.pallas_call(
        kernel,
        out_shape=(
            pltpu.VMEM((FEATS, COLS), BF16),
            pltpu.VMEM((RANK, COLS), F32),
            pltpu.VMEM((FEATS, COLS), F32),
            pltpu.VMEM((FEATS, 128), BF16),
            pltpu.VMEM((RANK, 6 * RANK), BF16),
            pltpu.VMEM((NY, 8, COLS), F32),
        ),
        in_specs=[any_spec] * 4,
        out_specs=(vmem_spec,) * 6,
        scratch_shapes=[
            pltpu.VMEM((L, TOK, FEATS), BF16),
            pltpu.VMEM((L, TOK, COLS), BF16),
            pltpu.VMEM((FEATS, COLS), BF16),
            pltpu.VMEM((L, RANK, COLS), F32),
            pltpu.VMEM((L, 3 * RANK, COLS), BF16),
            pltpu.VMEM((FEATS, COLS), F32),
            pltpu.VMEM((FEATS, 128), BF16),
            pltpu.VMEM((RANK, 6 * RANK), BF16),
            pltpu.VMEM((NY, 8, COLS), F32),
            pltpu.VMEM((L, FEATS, COLS), BF16),
            pltpu.VMEM((L, FEATS, COLS), BF16),
            pltpu.VMEM((L, 2, RANK, HALF), F32),
            pltpu.VMEM((L, RANK, HALF), F32),
            pltpu.VMEM((L, 3 * RANK, HALF), BF16),
            pltpu.VMEM((L, SUB, NBLK, ROWS, BLK), F32),
            pltpu.VMEM((L, SUB, OWN, ROWS, BLK), F32),
            pltpu.VMEM((L, SUB, OWN, ROWS, BLK), F32),
            pltpu.VMEM((L, SUB, NX * NY - 1, ROWS, BLK), F32),
            pltpu.VMEM((L, SUB, NZ, ROWS, BLK), F32),
            pltpu.VMEM((L, SUB, NBLK, ROWS, BLK), F32),
            pltpu.VMEM((L, 3 * RANK, FEATS), BF16),
            pltpu.VMEM((L, NY, 8, COLS), F32),
            pltpu.VMEM((L, NY - 1, 8, COLS), F32),
            pltpu.VMEM((L, NZ, 8, COLS), F32),
            pltpu.SemaphoreType.DMA((15,)),
        ]
        + [pair] * 2
        + [four] * 10
        + [pair] * 6,
        compiler_params=pltpu.CompilerParams(
            collective_id=0, has_side_effects=True, vmem_limit_bytes=54 * 1024 * 1024
        ),
        cost_estimate=pl.CostEstimate(flops=8_400_000_000, bytes_accessed=35_000_000, transcendentals=0),
    )(saved_inputs, kv_cotangent, error_buffer, q_start)
    return pl.pallas_call(
        finish,
        out_shape=(
            jax.ShapeDtypeStruct((1, L, FEATS, COLS), BF16),
            jax.ShapeDtypeStruct((L, RANK, COLS), F32),
        ),
        in_specs=[vmem_spec] * 6,
        out_specs=(any_spec, vmem_spec),
        scratch_shapes=[pltpu.VMEM((FEATS, COLS), BF16), pltpu.SemaphoreType.DMA((1 + FEATS // 512,))],
        compiler_params=pltpu.CompilerParams(vmem_limit_bytes=16 * 1024 * 1024),
        cost_estimate=pl.CostEstimate(flops=240_000_000, bytes_accessed=4_000_000, transcendentals=0),
    )(*(pltpu.with_memory_space_constraint(a, pltpu.VMEM) for a in held))


def solution(mesh):
    placed = (
        P(None, "dp", None),
        P(None, "dp", "tensor"),
        P("dp", None, None, "tensor"),
        P(None, None, "tensor"),
    )
    return jax.shard_map(
        body,
        mesh=mesh,
        in_specs=placed,
        out_specs=(P("dp", None, None, "tensor"), P(None, None, "tensor")),
        check_vma=False,
    )
```

```python
import functools

import jax
import jax.numpy as jnp
from jax import lax
from jax.experimental import pallas as pl
from jax.experimental.pallas import tpu as pltpu
from jax.sharding import PartitionSpec as P

MESH = pl.DeviceIdType.MESH
F32, BF16 = jnp.float32, jnp.bfloat16
FEATS, RANK, LAYERS, TOK, COLS = 3584, 32, 2, 2048, 256
NZ, NY, NX = 8, 4, 4
HALF = TOK // 2
BLK = 128
NBLK = FEATS // BLK
OWN = NBLK // 2
GRAD_F = 512


def mm(a, b, ca=1, cb=0):
    return lax.dot_general(a, b, (((ca,), (cb,)), ((), ())), preferred_element_type=F32)


def split3(v):
    hi = v.astype(BF16)
    rest = v - hi.astype(F32)
    mid = rest.astype(BF16)
    lo = (rest - mid.astype(F32)).astype(BF16)
    return jnp.concatenate([hi, mid, lo], axis=0)


def fold3(r):
    return r[0:RANK] + r[RANK : 2 * RANK] + r[2 * RANK : 3 * RANK]


SUB = 1
ROWS = RANK // SUB
CUT = 3 * GRAD_F
XY_ORDER = sorted(range(1, NX * NY), key=lambda j: -(min(j % NX, NX - j % NX) + min(j // NX, NY - j // NX)))
Z_ORDER = sorted(range(1, NZ), key=lambda j: -min(j, NZ - j))
Y_ORDER = (2, 1, 3)


def new_error(m, ot, q, rows):
    top = q.astype(BF16)
    rest = (q - top.astype(F32)).astype(BF16)
    return (m[rows, :] - mm(ot[rows, :], jnp.concatenate([top, rest, top, rest], axis=0))).astype(BF16)


def wide_left(v):
    t = split3(v)
    top, mid, low = t[0:RANK], t[RANK : 2 * RANK], t[2 * RANK : 3 * RANK]
    return jnp.concatenate([top, top, top, mid, mid, low], axis=1)


def right_of(top, mid, low):
    return jnp.concatenate([top, mid, low, top, mid, top], axis=0)


def q_from(gl, qt):
    t = split3(jnp.concatenate([qt[i] for i in range(NY)], axis=0))
    return mm(gl[...], right_of(t[0:RANK], t[RANK : 2 * RANK], t[2 * RANK : 3 * RANK]))


def kernel(
    s_hbm, k_hbm, e_hbm, q_hbm, err0, q0, m1, ot1, gl1, qt1,
    s, k, e1, qv, q3, m0, ot0, gl0, qt0, hi, lo, zl, zr, z3, pp, cr, ps, xr, zs, pf, p3, ub, yr, zq,
    hs, z_s, z_r, c_s, c_r, xy_s, xy_r, zz_s, zz_r, ag_s, ag_r, ac_s, ac_r, y1_s, y1_r, qz_s, qz_r, y2_s, y2_r,
):
    e, m, ot, gl, qt = (err0, e1), (m0, m1), (ot0, ot1), (gl0, gl1), (qt0, qt1)
    dp, t = lax.axis_index("dp"), lax.axis_index("tensor")
    z, y, x, c = dp // NY, dp % NY, t // 2, t % 2
    xy = y * NX + x

    def dev(z_, y_, x_, c_):
        return (z_ * NY + y_, x_ * 2 + c_)

    partner = dev(z, y, x, 1 - c)

    def xy_peer(j):
        return (y + j // NX) % NY, (x + j % NX) % NX

    def remote(src, dst, ss, rs, device):
        return pltpu.make_async_remote_copy(
            src_ref=src, dst_ref=dst, send_sem=ss, recv_sem=rs, device_id=device, device_id_type=MESH
        )

    def wait_recv(ref, ss, rs):
        remote(ref, ref, ss, rs, partner).wait_recv()

    def wait_send(ref, ss, rs):
        remote(ref, ref, ss, rs, partner).wait_send()

    barrier = pltpu.get_barrier_semaphore()
    pl.semaphore_signal(barrier, inc=1, device_id=partner, device_id_type=MESH)

    def greet_z(j, _):
        pl.semaphore_signal(barrier, inc=1, device_id=dev((z + j) % NZ, y, x, c), device_id_type=MESH)
        return 0

    def greet_xy(j, _):
        ny, nx = xy_peer(j)
        pl.semaphore_signal(barrier, inc=1, device_id=dev(z, ny, nx, c), device_id_type=MESH)
        return 0

    lax.fori_loop(1, NZ, greet_z, 0)
    lax.fori_loop(1, NX * NY, greet_xy, 0)

    def token_copy(hbm, vmem, l, part, cols, sem):
        rows = pl.ds(pl.multiple_of((c if part == 0 else 1 - c) * HALF, HALF), HALF)
        return pltpu.make_async_copy(hbm.at[l, rows, cols], vmem.at[l, pl.ds(part * HALF, HALF), cols], sem)

    def side_cols(side):
        return pl.ds(pl.multiple_of(side * (FEATS // 2), FEATS // 2), FEATS // 2)

    cq = pltpu.make_async_copy(q_hbm, qv, hs.at[0])
    ck = [[token_copy(k_hbm, k, l, h, pl.ds(0, COLS), hs.at[1 + 2 * l + h]) for h in range(2)] for l in range(LAYERS)]
    ce = [pltpu.make_async_copy(e_hbm.at[0, l], e[l], hs.at[5 + l]) for l in range(LAYERS)]
    own = [
        [token_copy(s_hbm, s, l, 0, side_cols(side), hs.at[7 + 2 * l + i]) for i, side in enumerate((1 - c, c))]
        for l in range(LAYERS)
    ]
    rest = [
        [token_copy(s_hbm, s, l, 1, cols, hs.at[11 + 2 * l + i]) for i, cols in enumerate((pl.ds(0, CUT), pl.ds(CUT, FEATS - CUT)))]
        for l in range(LAYERS)
    ]
    cq.start()
    for l in range(LAYERS):
        ck[l][0].start()
        ck[l][1].start()
    ce[0].start()
    ce[1].start()

    cq.wait()
    for l in range(LAYERS):
        q3[l] = split3(qv[l])
    for l in range(LAYERS):
        ck[l][0].wait()
        ck[l][1].wait()
        own[0][l].start()
        for h in range(2):
            zl[l, h] = fold3(mm(q3[l], k[l, pl.ds(h * HALF, HALF), :], 1, 1))

    def error_part(l):
        ce[l].wait()
        for i in range(4):
            r = fold3(mm(q3[l], e[l][pl.ds(i * 896, 896), :], 1, 1))
            for h in range(SUB):
                for j in range(7):
                    pp[l, h, i * 7 + j] = r[h * ROWS : (h + 1) * ROWS, j * BLK : (j + 1) * BLK]

    error_part(0)
    own[1][0].start()
    error_part(1)

    pl.semaphore_wait(barrier, 1 + (NZ - 1) + (NX * NY - 1))
    for l in range(LAYERS):
        remote(zl.at[l, 1], zr.at[l], z_s.at[l], z_r.at[l], partner).start()

    def p_blocks(l, side):
        for i in range(2):
            b0 = side * OWN + i * 7
            f0 = pl.multiple_of(b0 * BLK, BLK)
            r = fold3(mm(z3[l], s[l, pl.ds(0, HALF), pl.ds(f0, 7 * BLK)]))
            for h in range(SUB):
                for j in range(7):
                    pp[l, h, b0 + j] += r[h * ROWS : (h + 1) * ROWS, j * BLK : (j + 1) * BLK]

    def p_other(l):
        wait_recv(zr.at[l], z_s.at[l], z_r.at[l])
        z3[l] = split3(zl[l, 0] + zr[l])
        own[l][0].wait()
        p_blocks(l, 1 - c)
        for h in range(SUB):
            remote(pp.at[l, h, pl.ds((1 - c) * OWN, OWN)], cr.at[l, h], c_s.at[l, h], c_r.at[l, h], partner).start()

    def p_mine(l):
        own[l][1].wait()
        if l == 0:
            own[1][1].start()
        else:
            rest[0][0].start()
            rest[0][1].start()
        p_blocks(l, c)

    def mine(l):
        return xy - 2 * l

    def owner(l):
        return (mine(l) >= 0) & (mine(l) < OWN)

    def add_cores(l, h):
        wait_recv(cr.at[l, h], c_s.at[l, h], c_r.at[l, h])
        for b in range(OWN):
            ps[l, h, b] = pp[l, h, c * OWN + b] + cr[l, h, b]
        for j in XY_ORDER:
            ny, nx = xy_peer(j)
            b = ny * NX + nx - 2 * l

            @pl.when((b >= 0) & (b < OWN))
            def _():
                remote(ps.at[l, h, b], xr.at[l, h, j - 1], xy_s.at[l, h], xy_r.at[l, h], dev(z, ny, nx, c)).start()

    def add_plane(l, h):
        @pl.when(owner(l))
        def _():
            wait_recv(xr.at[l, h], xy_s.at[l, h], xy_r.at[l, h])
            total = ps[l, h, mine(l)]
            for j in range(NX * NY - 1):
                total = total + xr[l, h, j]
            zs[l, h, z] = total
            for j in Z_ORDER:
                there = dev((z + j) % NZ, y, x, c)
                remote(zs.at[l, h, z], zs.at[l, h, z], zz_s.at[l, h], zz_r.at[l, h], there).start()

    def add_z(l, h):
        @pl.when(owner(l))
        def _():
            wait_recv(zs.at[l, h, pl.ds(0, NZ - 1)], zz_s.at[l, h], zz_r.at[l, h])
            total = zs[l, h, 0]
            for j in range(1, NZ):
                total = total + zs[l, h, j]
            b = c * OWN + mine(l)
            pf[l, h, b] = total
            for j in XY_ORDER:
                ny, nx = xy_peer(j)
                remote(pf.at[l, h, b], pf.at[l, h, b], ag_s.at[l, h], ag_r.at[l, h], dev(z, ny, nx, c)).start()

    def share_core(l, h):
        @pl.when(owner(l))
        def _():
            wait_recv(pf.at[l, h, pl.ds(0, OWN - 1)], ag_s.at[l, h], ag_r.at[l, h])

        @pl.when(jnp.logical_not(owner(l)))
        def _():
            wait_recv(pf.at[l, h, pl.ds(0, OWN)], ag_s.at[l, h], ag_r.at[l, h])

        half = pf.at[l, h, pl.ds(c * OWN, OWN)]
        remote(half, half, ac_s.at[l, h], ac_r.at[l, h], partner).start()

    def grad(l, i0, i1):
        for i in range(i0, i1):
            rows = pl.ds(i * GRAD_F, GRAD_F)
            if i == 0 or i * GRAD_F == CUT:
                part = 0 if i == 0 else 1
                rest[l][part].wait()
                if l == 0:
                    rest[1][part].start()
            g = mm(s[l, :, rows], k[l], 0, 0) + e[l][rows, :].astype(F32)
            m[l][rows, :] = g
            top = g.astype(BF16)
            hi[l, rows, :] = top
            lo[l, rows, :] = (g - top.astype(F32)).astype(BF16)

    def q_half(l, side):
        u = jnp.zeros((RANK, COLS), F32)
        for i in range(OWN // 2):
            b0 = side * OWN + 2 * i
            rows = pl.ds(pl.multiple_of(b0 * BLK, 2 * BLK), 2 * BLK)
            halves = [jnp.concatenate([pf[l, h, b0], pf[l, h, b0 + 1]], axis=1) for h in range(SUB)]
            terms = split3(jnp.concatenate(halves, axis=0))
            p3[l, :, rows] = terms
            r = fold3(mm(terms, hi[l, rows, :]))
            r2 = mm(terms[0 : 2 * RANK], lo[l, rows, :])
            u = u + (r + (r2[0:RANK] + r2[RANK : 2 * RANK]))
        return u

    def q_send(l, u):
        for i in range(NY):
            ub[l, i] = u[8 * i : 8 * i + 8]

        for j in Y_ORDER:
            ny = (y + j) % NY
            remote(ub.at[l, ny], yr.at[l, j - 1], y1_s.at[l], y1_r.at[l], dev(z, ny, x, c)).start()

    def q_add_y(l):
        wait_recv(yr.at[l], y1_s.at[l], y1_r.at[l])
        zq[l, z] = ub[l, y] + yr[l, 0] + yr[l, 1] + yr[l, 2]
        for j in Z_ORDER:
            remote(zq.at[l, z], zq.at[l, z], qz_s.at[l], qz_r.at[l], dev((z + j) % NZ, y, x, c)).start()

    def q_add_z(l):
        wait_recv(zq.at[l, pl.ds(0, NZ - 1)], qz_s.at[l], qz_r.at[l])
        total = zq[l, 0]
        for j in range(1, NZ):
            total = total + zq[l, j]
        qt[l][y] = total * (1.0 / (NZ * NY))
        for j in Y_ORDER:
            remote(qt[l].at[y], qt[l].at[y], y2_s.at[l], y2_r.at[l], dev(z, (y + j) % NY, x, c)).start()

    def gram(l):
        g = jnp.zeros((3 * RANK, 3 * RANK), F32)
        for i in range(FEATS // 512):
            terms = p3[l, :, pl.ds(i * 512, 512)]
            g = g + mm(terms, terms, 1, 1)
        g = fold3(g)
        return g[:, 0:RANK] + g[:, RANK : 2 * RANK] + g[:, 2 * RANK : 3 * RANK]

    def inverse_factors(grams):
        rows = lax.broadcasted_iota(jnp.int32, (RANK, 1), 0)
        eye = (rows == lax.broadcasted_iota(jnp.int32, (RANK, RANK), 1)).astype(F32)
        work = [jnp.concatenate([g, eye], axis=1) for g in grams]
        for j in range(RANK):
            for n, a in enumerate(work):
                inv = lax.rsqrt(a[j : j + 1, j : j + 1])
                row = a[j : j + 1, :] * inv
                col = jnp.where(rows > j, a[:, j : j + 1] * inv, 0.0)
                work[n] = jnp.where(rows == j, row, a - col * row)
        return [a[:, RANK : 2 * RANK] for a in work]

    def ortho(l):
        for i in range(FEATS // 512):
            rows = pl.ds(i * 512, 512)
            o = mm(gl[l][...], right_of(*(p3[l, pl.ds(n * RANK, RANK), rows] for n in range(3))))
            o_top = o.astype(BF16)
            o_low = (o - o_top.astype(F32)).astype(BF16)
            ot[l][rows, :] = jnp.concatenate([o_top, o_top, o_low, o_low], axis=0).T

    pairs = [(l, h) for l in range(LAYERS) for h in range(SUB)]
    for l in range(LAYERS):
        p_other(l)
        p_mine(l)
        for h in range(SUB):
            add_cores(l, h)
    grad(0, 0, 5)
    for l, h in pairs:
        add_plane(l, h)
    grad(0, 5, 7)
    grad(1, 0, 3)
    for l, h in pairs:
        add_z(l, h)
    grad(1, 3, 7)
    for l, h in pairs:
        share_core(l, h)
    own_q = [q_half(l, c) for l in range(LAYERS)]
    for l in range(LAYERS):
        for h in range(SUB):
            wait_recv(pf.at[l, h, pl.ds(0, OWN)], ac_s.at[l, h], ac_r.at[l, h])
        q_send(l, own_q[l] + q_half(l, 1 - c))
    grams = [gram(l) for l in range(LAYERS)]
    for l in range(LAYERS):
        q_add_y(l)
    for l, inverse in enumerate(inverse_factors(grams)):
        gl[l][...] = wide_left(inverse)
    for l in range(LAYERS):
        q_add_z(l)
    ortho(0)
    ortho(1)
    wait_recv(qt[0].at[pl.ds(0, NY - 1)], y2_s.at[0], y2_r.at[0])
    q0[...] = q_from(gl[0], qt[0])
    for i in range(FEATS // 512):
        rows = pl.ds(i * 512, 512)
        err0[rows, :] = new_error(m[0], ot[0], q0[...], rows)
    wait_recv(qt[1].at[pl.ds(0, NY - 1)], y2_s.at[1], y2_r.at[1])

    for l in range(LAYERS):
        wait_send(zl.at[l, 1], z_s.at[l], z_r.at[l])
        for h in range(SUB):
            wait_send(cr.at[l, h], c_s.at[l, h], c_r.at[l, h])

            @pl.when(owner(l))
            def _():
                wait_send(ps.at[l, h, pl.ds(0, OWN - 1)], xy_s.at[l, h], xy_r.at[l, h])
                wait_send(zs.at[l, h, pl.ds(0, NZ - 1)], zz_s.at[l, h], zz_r.at[l, h])
                wait_send(pf.at[l, h, pl.ds(0, NX * NY - 1)], ag_s.at[l, h], ag_r.at[l, h])

            @pl.when(jnp.logical_not(owner(l)))
            def _():
                wait_send(ps.at[l, h, pl.ds(0, OWN)], xy_s.at[l, h], xy_r.at[l, h])

            wait_send(pf.at[l, h, pl.ds(0, OWN)], ac_s.at[l, h], ac_r.at[l, h])
        wait_send(ub.at[l, pl.ds(0, NY - 1)], y1_s.at[l], y1_r.at[l])
        wait_send(zq.at[l, pl.ds(0, NZ - 1)], qz_s.at[l], qz_r.at[l])
        wait_send(qt[l].at[pl.ds(0, NY - 1)], y2_s.at[l], y2_r.at[l])


def finish(err0, q0, m1, ot1, gl1, qt1, err_hbm, qf_hbm, out, qf, sems):
    first = pltpu.make_async_copy(err0, err_hbm.at[0, 0], sems.at[0])
    first.start()
    copies = [first]
    q = q_from(gl1, qt1)
    qf[0] = q0[...]
    qf[1] = q
    copies.append(pltpu.make_async_copy(qf, qf_hbm, sems.at[1]))
    copies[-1].start()
    for i in range(FEATS // 512):
        rows = pl.ds(i * 512, 512)
        out[rows, :] = new_error(m1, ot1, q, rows)
        copies.append(pltpu.make_async_copy(out.at[rows], err_hbm.at[0, 1, rows], sems.at[2 + i]))
        copies[-1].start()
    for copy in copies:
        copy.wait()


def body(saved_inputs, kv_cotangent, error_buffer, q_start):
    L = LAYERS
    pair, four = pltpu.SemaphoreType.DMA((L,)), pltpu.SemaphoreType.DMA((L, SUB))
    any_spec, vmem_spec = pl.BlockSpec(memory_space=pl.ANY), pl.BlockSpec(memory_space=pltpu.VMEM)
    held = pl.pallas_call(
        kernel,
        out_shape=(
            pltpu.VMEM((FEATS, COLS), BF16),
            pltpu.VMEM((RANK, COLS), F32),
            pltpu.VMEM((FEATS, COLS), F32),
            pltpu.VMEM((FEATS, 128), BF16),
            pltpu.VMEM((RANK, 6 * RANK), BF16),
            pltpu.VMEM((NY, 8, COLS), F32),
        ),
        in_specs=[any_spec] * 4,
        out_specs=(vmem_spec,) * 6,
        scratch_shapes=[
            pltpu.VMEM((L, TOK, FEATS), BF16),
            pltpu.VMEM((L, TOK, COLS), BF16),
            pltpu.VMEM((FEATS, COLS), BF16),
            pltpu.VMEM((L, RANK, COLS), F32),
            pltpu.VMEM((L, 3 * RANK, COLS), BF16),
            pltpu.VMEM((FEATS, COLS), F32),
            pltpu.VMEM((FEATS, 128), BF16),
            pltpu.VMEM((RANK, 6 * RANK), BF16),
            pltpu.VMEM((NY, 8, COLS), F32),
            pltpu.VMEM((L, FEATS, COLS), BF16),
            pltpu.VMEM((L, FEATS, COLS), BF16),
            pltpu.VMEM((L, 2, RANK, HALF), F32),
            pltpu.VMEM((L, RANK, HALF), F32),
            pltpu.VMEM((L, 3 * RANK, HALF), BF16),
            pltpu.VMEM((L, SUB, NBLK, ROWS, BLK), F32),
            pltpu.VMEM((L, SUB, OWN, ROWS, BLK), F32),
            pltpu.VMEM((L, SUB, OWN, ROWS, BLK), F32),
            pltpu.VMEM((L, SUB, NX * NY - 1, ROWS, BLK), F32),
            pltpu.VMEM((L, SUB, NZ, ROWS, BLK), F32),
            pltpu.VMEM((L, SUB, NBLK, ROWS, BLK), F32),
            pltpu.VMEM((L, 3 * RANK, FEATS), BF16),
            pltpu.VMEM((L, NY, 8, COLS), F32),
            pltpu.VMEM((L, NY - 1, 8, COLS), F32),
            pltpu.VMEM((L, NZ, 8, COLS), F32),
            pltpu.SemaphoreType.DMA((15,)),
        ]
        + [pair] * 2
        + [four] * 10
        + [pair] * 6,
        compiler_params=pltpu.CompilerParams(
            collective_id=0, has_side_effects=True, vmem_limit_bytes=54 * 1024 * 1024
        ),
        cost_estimate=pl.CostEstimate(flops=8_400_000_000, bytes_accessed=35_000_000, transcendentals=0),
    )(saved_inputs, kv_cotangent, error_buffer, q_start)
    return pl.pallas_call(
        finish,
        out_shape=(
            jax.ShapeDtypeStruct((1, L, FEATS, COLS), BF16),
            jax.ShapeDtypeStruct((L, RANK, COLS), F32),
        ),
        in_specs=[vmem_spec] * 6,
        out_specs=(any_spec, any_spec),
        scratch_shapes=[
            pltpu.VMEM((FEATS, COLS), BF16),
            pltpu.VMEM((L, RANK, COLS), F32),
            pltpu.SemaphoreType.DMA((2 + FEATS // 512,)),
        ],
        compiler_params=pltpu.CompilerParams(vmem_limit_bytes=16 * 1024 * 1024),
        cost_estimate=pl.CostEstimate(flops=240_000_000, bytes_accessed=4_000_000, transcendentals=0),
    )(*(pltpu.with_memory_space_constraint(a, pltpu.VMEM) for a in held))


def solution(mesh):
    placed = (
        P(None, "dp", None),
        P(None, "dp", "tensor"),
        P("dp", None, None, "tensor"),
        P(None, None, "tensor"),
    )
    return jax.shard_map(
        body,
        mesh=mesh,
        in_specs=placed,
        out_specs=(P("dp", None, None, "tensor"), P(None, None, "tensor")),
        check_vma=False,
    )
```
